32 devices in a mesh: fsdp: 8 (over z, x), rep: 4 (over y, core).
Axes of the slice: x: 2, y: 2, z: 4, core: 2. Of those that a mesh axis runs over, the one named last changes fastest.
Arguments:
- grad: float32 [4, 256, 8192], P('rep', 'fsdp'), may hold values from -45 to 45
- z_params: float32 [4, 256, 8192], P('rep', 'fsdp'), may hold values from -6 to 6
- x_params: float32 [4, 256, 8192], P('rep', 'fsdp'), may hold values from -6 to 6
- owner: int32 [8], replicated, may hold values from 0 to 7, each once
- stat_left: float32 [8, 1024, 1024], P('fsdp', 'rep'), may hold values from -6 to 6
- stat_right: float32 [8, 1024, 1024], P('fsdp', 'rep'), may hold values from -6 to 6
- root_left: bfloat16 [8, 1024, 1024], P('fsdp', 'rep'), may hold values from -0.1875 to 0.1875
- root_right: bfloat16 [8, 1024, 1024], P('fsdp', 'rep'), may hold values from -0.1875 to 0.1875
Outputs:
- z_new: float32 [4, 256, 8192], P('rep', 'fsdp')
- x_new: float32 [4, 256, 8192], P('rep', 'fsdp')
- y_new: bfloat16 [4, 256, 8192], P('rep', 'fsdp')
- left_new: float32 [8, 1024, 1024], P('fsdp', 'rep')
- right_new: float32 [8, 1024, 1024], P('fsdp', 'rep')
The draws below stay inside these ranges and needn't reach their ends.
Inputs may be any that keep to these rules, and one draw needn't show every extreme that they name: `owner`: each fsdp index owns exactly one block.
All inputs are finite; a program needn't handle non-finite values.
Results may differ from the reference program's by a relative error of at most 0.0025.
Values may be sent and summed in bfloat16 or wider, within the bound.
No kernel may reach another device: no remote copies, remote signals or barrier semaphores. Data moves between devices by JAX's collectives and lax.ppermute only.
A program may use at most 320 MiB of HBM per device.

```python
import math
import jax
import jax.numpy as jnp
from jax import lax

BLK = 1024
NB = 8
COLS = 8192
Q = 256
N_REP = 4


def draw_grad(key, part):
    key = jax.random.fold_in(key, 11)
    key_base, key_rows, key_cols = jax.random.split(key, 3)
    shape = (N_REP, Q, COLS)
    base = jnp.clip(jax.random.normal(key_base, shape, jnp.float32), -5.0, 5.0)
    lower, upper = (0.3, 3.0)
    row_scale = jnp.exp(jax.random.uniform(key_rows, (N_REP, Q, 1), jnp.float32, math.log(lower), math.log(upper)))
    col_scale = jnp.exp(jax.random.uniform(key_cols, (1, 1, COLS), jnp.float32, math.log(lower), math.log(upper)))
    return (base * row_scale * col_scale).astype(jnp.float32)


def levels(stream_key, extent, shards, least, top_value):
    level = 1.0
    for dim, shards_of in shards:
        heights = jax.random.uniform(jax.random.fold_in(jax.random.fold_in(stream_key, 6), dim), (shards_of,), jnp.float32, least / len(shards), top_value / len(shards))
        level = level * jnp.repeat(jnp.exp(heights), extent[dim] // shards_of).reshape((-1,) + (1,) * (len(extent) - 1 - dim))
    return level


def centred(stream_key, extent, width, limit, cuts=(), held_as=jnp.bfloat16):
    drawn = jax.random.normal(stream_key, extent, jnp.float32) * width
    if len(cuts) > 0:
        drawn = levels(stream_key, extent, cuts, -0.22, 0.18) * drawn
    return jnp.clip(drawn, min=-limit, max=limit).astype(held_as)


def setup_inputs(seed: int = 0) -> dict:
    key_of = jax.random.split(jax.random.key(seed), 9)
    grad = draw_grad(jax.random.fold_in(key_of[8], 71), 0)
    z_params = centred(key_of[1], (N_REP, Q, COLS), 1.0, 6.0, ((0, 4), (1, 8)), jnp.float32)
    x_params = centred(key_of[2], (N_REP, Q, COLS), 1.0, 6.0, ((0, 4), (1, 8)), jnp.float32)
    owner = jax.random.permutation(key_of[3], NB).astype(jnp.int32)
    stat_left = centred(key_of[4], (NB, BLK, BLK), 1.0, 6.0, ((0, 8), (1, 4)), jnp.float32)
    stat_right = centred(key_of[5], (NB, BLK, BLK), 1.0, 6.0, ((0, 8), (1, 4)), jnp.float32)
    root_left = centred(key_of[6], (NB, BLK, BLK), BLK ** -0.5, 0.1875, ((0, 8), (1, 4)))
    root_right = centred(key_of[7], (NB, BLK, BLK), BLK ** -0.5, 0.1875, ((0, 8), (1, 4)))
    return {"grad": grad, "z_params": z_params, "x_params": x_params, "owner": owner, "stat_left": stat_left, "stat_right": stat_right, "root_left": root_left, "root_right": root_right}


def reference(grad, z_params, x_params, owner, stat_left, stat_right, root_left, root_right):
    whole = grad.reshape(BLK, COLS)
    inverse = jnp.argsort(owner).astype(jnp.int32)
    count = owner.shape[0]

    def one_block(slot):
        block_id = inverse[slot]
        block = lax.dynamic_slice_in_dim(whole, block_id * BLK, BLK, 1)
        left = 0.95 * stat_left[slot] + 0.05 / BLK * jnp.dot(block, block.T, precision=lax.Precision.HIGHEST)
        right = 0.95 * stat_right[slot] + 0.05 / BLK * jnp.dot(block.T, block, precision=lax.Precision.HIGHEST)
        left_prod = jnp.dot(root_left[slot], block.astype(jnp.bfloat16), preferred_element_type=jnp.float32).astype(jnp.bfloat16)
        precond = jnp.dot(left_prod, root_right[slot], preferred_element_type=jnp.float32)
        scale = jnp.sqrt(jnp.mean(block * block)) * lax.rsqrt(jnp.mean(precond * precond) + 1e-06)
        return (left, right, (scale * precond).astype(jnp.bfloat16))
    left_new, right_new, directions = lax.map(one_block, jnp.arange(count, dtype=jnp.int32))
    ordered = directions[owner]
    flat_dir = jnp.transpose(ordered, (1, 0, 2)).reshape(grad.shape)
    z_new = z_params - 0.2 * flat_dir.astype(jnp.float32)
    x_new = 0.75 * x_params + 0.25 * z_new
    y_new = (0.1 * z_new + 0.9 * x_new).astype(jnp.bfloat16)
    return (z_new, x_new, y_new, left_new, right_new)
```

```python
import functools

import jax
import jax.numpy as jnp
from jax import lax
from jax.experimental import pallas as pl
from jax.experimental.pallas import tpu as pltpu
from jax.sharding import PartitionSpec as P

F32 = jnp.float32
BF16 = jnp.bfloat16
ANY = pl.BlockSpec(memory_space=pl.ANY)
VMEM = pl.BlockSpec(memory_space=pltpu.VMEM)
HBM = pl.BlockSpec(memory_space=pltpu.HBM)
MIB = 1 << 20


def params(mib):
    return pltpu.CompilerParams(vmem_limit_bytes=mib * MIB)


def cost(flops, moved):
    return pl.CostEstimate(flops=flops, bytes_accessed=moved, transcendentals=0)


def swap(x, axis, size, bit):
    return lax.ppermute(x, axis, [(i, i ^ bit) for i in range(size)])


def in_hbm(x):
    return pltpu.with_memory_space_constraint(x, pltpu.HBM)


def invert(owner_mem, block_mem, count):
    for b in range(count):
        block_mem[owner_mem[b]] = jnp.int32(b)


def route_kernel(owner_ref, grad_ref, *refs):
    outs, (owner_mem, block_mem, held, sems) = refs[:-4], refs[-4:]
    me = lax.axis_index("fsdp")
    count, rows, width = held.shape

    def load(b):
        start = b * width if isinstance(b, int) else pl.multiple_of(b * width, width)
        return pltpu.make_async_copy(
            grad_ref.at[:, pl.ds(start, width)], held.at[b], sems.at[b]
        )

    index = pltpu.make_async_copy(owner_ref, owner_mem, sems.at[count])
    index.start()
    for b in range(count):
        load(b).start()
    index.wait()
    invert(owner_mem, block_mem, count)
    for d in reversed(range(count)):
        b = block_mem[me ^ d]
        load(b).wait()
        outs[d][...] = held[b].astype(BF16)


def route(grad, owner, count):
    rows, width = grad.shape[0], grad.shape[1] // count
    return pl.pallas_call(
        route_kernel,
        out_shape=[jax.ShapeDtypeStruct((rows, width), BF16)] * count,
        in_specs=[HBM, HBM],
        out_specs=[VMEM] * count,
        scratch_shapes=[
            pltpu.SMEM((count,), jnp.int32),
            pltpu.SMEM((count,), jnp.int32),
            pltpu.VMEM((count, rows, width), F32),
            pltpu.SemaphoreType.DMA((count + 1,)),
        ],
        compiler_params=params(8),
        cost_estimate=cost(0, 6 * grad.size),
        name="route",
    )(in_hbm(owner), in_hbm(grad))


def local_call(kernel, shape, operands, name, *early):
    return pl.pallas_call(
        kernel,
        out_shape=jax.ShapeDtypeStruct(shape, BF16),
        in_specs=[VMEM] * len(operands) + [ANY] * len(early),
        out_specs=VMEM,
        compiler_params=params(8),
        cost_estimate=cost(0, 4 * shape[0] * shape[1]),
        name=name,
    )(*operands, *early)


FIRST = (0, 1, 4, 5)
SECOND = (2, 3, 6, 7)


def half_kernel(half_of, there, *refs):
    out_ref = refs[-1]
    rows = refs[0].shape[0]
    odd = lax.axis_index("fsdp") % 2
    for ref, d in zip(refs, there):
        place = half_of.index(d) // 2 * 2 + (odd ^ (d % 2))
        out_ref[pl.ds(pl.multiple_of(place * rows, rows), rows), :] = ref[...]


def half(got, half_of, there, *early):
    rows, width = got[0].shape
    kernel = functools.partial(half_kernel, half_of, there)
    return local_call(kernel, (4 * rows, width), [got[d] for d in there], "half", *early)


def join_kernel(first_ref, second_ref, *refs):
    out_ref = refs[-1]
    rows = first_ref.shape[0] // 2
    pair = lax.axis_index("fsdp") // 2
    for ref, half_of in ((first_ref, FIRST), (second_ref, SECOND)):
        for k in range(2):
            place = pl.multiple_of((pair ^ (half_of[2 * k] // 2)) * rows, rows)
            out_ref[pl.ds(place, rows), :] = ref[k * rows : (k + 1) * rows, :]


def join(first, second, *early):
    shape = (2 * first.shape[0], first.shape[1])
    return local_call(join_kernel, shape, (first, second), "join", *early)


def after(x, first):
    def kernel(x_ref, first_ref, out_ref):
        pass

    return pl.pallas_call(
        kernel,
        out_shape=jax.ShapeDtypeStruct(x.shape, x.dtype),
        in_specs=[ANY, ANY],
        out_specs=ANY,
        input_output_aliases={0: 0},
        compiler_params=params(1),
        cost_estimate=cost(0, 0),
        name="after",
    )(x, first)


def precond_kernel(members, left_ref, *refs):
    g_refs, r_refs = refs[:members], refs[members : 2 * members]
    out_ref, sums_ref, mid_ref = refs[-3:]
    member = lax.axis_index("rep")
    q = left_ref.shape[0]

    def part(ref, j):
        return ref[:, pl.ds(pl.multiple_of((member ^ j) * q, q), q)]

    def chain(ref, rights):
        total = jnp.dot(part(ref, 0), rights[0][...], preferred_element_type=F32)
        for j in range(1, members):
            total += jnp.dot(part(ref, j), rights[j][...], preferred_element_type=F32)
        return total

    mid_ref[...] = chain(left_ref, g_refs).astype(BF16)
    product = chain(mid_ref, r_refs)
    out_ref[...] = product
    own = g_refs[0][...].astype(F32)
    rows = lax.broadcasted_iota(jnp.int32, sums_ref.shape, 0)
    sums_ref[...] = jnp.where(rows == 0, jnp.sum(product * product), jnp.sum(own * own))


def precondition(left, blocks, rights, *early):
    q, width = left.shape
    members = len(blocks)
    return pl.pallas_call(
        functools.partial(precond_kernel, members),
        out_shape=[
            jax.ShapeDtypeStruct((q, width), F32),
            jax.ShapeDtypeStruct((8, 128), F32),
        ],
        in_specs=[VMEM] * (1 + 2 * members) + [ANY] * len(early),
        out_specs=[VMEM, VMEM],
        scratch_shapes=[pltpu.VMEM((q, width), BF16)],
        compiler_params=params(16),
        cost_estimate=cost(4 * q * width * width, 4 * width * width + 4 * q * width),
        name="precondition",
    )(left, *blocks, *rights, *early)


def scale_kernel(entries, count, n, product_ref, *refs):
    sums_refs, outs = refs[:n], refs[-count:]
    me = lax.axis_index("fsdp")
    rows = outs[0].shape[0]
    total = sum(ref[...] for ref in sums_refs) / entries
    scale = jnp.sqrt(total[1:2, :1]) * lax.rsqrt(total[:1, :1] + 1e-06)
    for d, out_ref in enumerate(outs):
        part = product_ref[pl.ds(pl.multiple_of((me ^ d) * rows, rows), rows), :]
        out_ref[...] = (scale * part).astype(BF16)


def rescale(product, sums, entries, count, *early):
    rows, width = product.shape[0] // count, product.shape[1]
    return pl.pallas_call(
        functools.partial(scale_kernel, entries, count, len(sums)),
        out_shape=[jax.ShapeDtypeStruct((rows, width), BF16)] * count,
        in_specs=[VMEM] * (1 + len(sums)) + [HBM] * len(early),
        out_specs=[VMEM] * count,
        compiler_params=params(8),
        cost_estimate=cost(product.size, 6 * product.size),
        name="rescale",
    )(product, *sums, *map(in_hbm, early))


def stats_kernel(members, rows_side, old_ref, *refs):
    g_refs = refs[:members]
    new_out, new_mem, sems = refs[members:]
    member = lax.axis_index("rep")
    q, width = old_ref.shape
    step = 0.05 / width
    strip = pl.ds(pl.multiple_of(member * q, q), q)
    stores = []
    for j in range(members):
        if rows_side:
            cols = pl.ds(pl.multiple_of((member ^ j) * q, q), q)
            product = lax.dot_general(
                g_refs[0][...], g_refs[j][...], (((1,), (1,)), ((), ())), preferred_element_type=F32
            )
        else:
            cols = pl.ds(j * q, q)
            product = sum(
                lax.dot_general(
                    g[:, strip], g[:, cols], (((0,), (0,)), ((), ())), preferred_element_type=F32
                )
                for g in g_refs
            )
        new_mem[j] = 0.95 * old_ref[:, cols] + step * product
        stores.append(pltpu.make_async_copy(new_mem.at[j], new_out.at[:, cols], sems.at[j]))
        stores[-1].start()
    for store in stores:
        store.wait()


def statistic(old, blocks, rows_side):
    q, width = old.shape
    members = len(blocks)
    return pl.pallas_call(
        functools.partial(stats_kernel, members, rows_side),
        out_shape=jax.ShapeDtypeStruct((q, width), F32),
        in_specs=[VMEM] * (1 + members),
        out_specs=HBM,
        scratch_shapes=[
            pltpu.VMEM((members, q, q), F32),
            pltpu.SemaphoreType.DMA((members,)),
        ],
        compiler_params=params(16),
        cost_estimate=cost(2 * q * width * width, 8 * q * width + 2 * width * width),
        name="left_statistic" if rows_side else "right_statistic",
    )(old, *blocks)


def stage_kernel(n, owner_ref, z_ref, x_ref, *refs):
    whole_refs, whole_outs = refs[:n], refs[-n - 6 : -6]
    z_out, x_out, block_out, owner_mem, block_mem, sems = refs[-6:]
    me = lax.axis_index("fsdp")
    count, _, width = z_out.shape
    index = pltpu.make_async_copy(owner_ref, owner_mem, sems.at[2, n])
    index.start()
    loads = [
        pltpu.make_async_copy(src, dst, sems.at[2, i])
        for i, (src, dst) in enumerate(zip(whole_refs, whole_outs))
    ]
    for load in loads:
        load.start()
    index.wait()
    invert(owner_mem, block_mem, count)
    for d in range(count):
        block = block_mem[me ^ d]
        block_out[pl.ds(d, 1), :] = jnp.full((1, block_out.shape[1]), block, jnp.int32)
        cols = pl.ds(pl.multiple_of(block * width, width), width)
        for i, (src, dst) in enumerate(((z_ref, z_out), (x_ref, x_out))):
            load = pltpu.make_async_copy(src.at[:, cols], dst.at[d], sems.at[i, d])
            load.start()
            loads.append(load)
    for load in loads:
        load.wait()


def stage(owner, z, x, wholes, count, *early):
    rows, width = z.shape[0], z.shape[1] // count
    n = len(wholes)
    moved = sum(2 * w.size * w.dtype.itemsize for w in wholes)
    return pl.pallas_call(
        functools.partial(stage_kernel, n),
        out_shape=[jax.ShapeDtypeStruct(w.shape, w.dtype) for w in wholes]
        + [
            jax.ShapeDtypeStruct((count, rows, width), F32),
            jax.ShapeDtypeStruct((count, rows, width), F32),
            jax.ShapeDtypeStruct((count, 128), jnp.int32),
        ],
        in_specs=[HBM] * (3 + n) + [ANY] * len(early),
        out_specs=[VMEM] * (n + 3),
        scratch_shapes=[
            pltpu.SMEM((count,), jnp.int32),
            pltpu.SMEM((count,), jnp.int32),
            pltpu.SemaphoreType.DMA((3, count)),
        ],
        compiler_params=params(8),
        cost_estimate=cost(0, 16 * z.size + moved),
        name="stage",
    )(*[in_hbm(a) for a in (owner, z, x, *wholes)], *early)


def update_kernel(distances, fresh, block_ref, z_ref, x_ref, *refs):
    n = len(distances)
    back, outs = refs[:n], refs[n : n + 3] if fresh else refs[n + 3 : n + 6]
    z_mem, x_mem, y_mem, sems = refs[-4:]
    width = z_ref.shape[2]
    blocks = [block_ref[d, 0] for d in distances]
    stores = []
    for k, d in enumerate(distances):
        z_new = z_ref[d] - 0.2 * back[k][...].astype(F32)
        x_new = 0.75 * x_ref[d] + 0.25 * z_new
        z_mem[k] = z_new
        x_mem[k] = x_new
        y_mem[k] = (0.1 * z_new + 0.9 * x_new).astype(BF16)
        cols = pl.ds(pl.multiple_of(blocks[k] * width, width), width)
        for i, mem in enumerate((z_mem, x_mem, y_mem)):
            store = pltpu.make_async_copy(mem.at[k], outs[i].at[:, cols], sems.at[i, k])
            store.start()
            stores.append(store)
    for store in stores:
        store.wait()


def update(block, z, x, back, distances, held=None):
    count, rows, width = z.shape
    flat = (rows, count * width)
    n = len(distances)
    fresh = held is None
    return pl.pallas_call(
        functools.partial(update_kernel, distances, fresh),
        out_shape=[
            jax.ShapeDtypeStruct(flat, F32),
            jax.ShapeDtypeStruct(flat, F32),
            jax.ShapeDtypeStruct(flat, BF16),
        ],
        in_specs=[VMEM] * (3 + n) + ([] if fresh else [HBM] * 3),
        out_specs=[HBM] * 3,
        input_output_aliases={} if fresh else {3 + n + i: i for i in range(3)},
        scratch_shapes=[
            pltpu.VMEM((n, rows, width), F32),
            pltpu.VMEM((n, rows, width), F32),
            pltpu.VMEM((n, rows, width), BF16),
            pltpu.SemaphoreType.DMA((3, n)),
        ],
        compiler_params=params(16),
        cost_estimate=cost(8 * n * rows * width, 20 * n * rows * width),
        name="update",
    )(block, z, x, *[back[d] for d in distances], *([] if fresh else held))


def gather_members(own, members):
    bit = members // 2
    got = {0: own}
    while bit:
        for known in list(got):
            got[known ^ bit] = swap(got[known], "rep", members, bit)
        bit //= 2
    return [got[j] for j in range(members)]


def eight_by_four(flat, z, x, owner, stat_left, stat_right, root_left, root_right, count, members):
    def send(piece, d):
        return swap(piece, "fsdp", count, d)

    def far(piece):
        return swap(piece, "rep", members, 2)

    def sibling(piece):
        return swap(piece, "rep", members, 1)

    entries = float(stat_left.shape[1] ** 2)
    right_far = far(root_right)
    piece = route(flat, owner, count)
    got = {0: piece[0]}
    for d in (4, 5, 3, 1):
        got[d] = send(piece[d], d)
    got[2] = send(after(piece[2], got[3]), 2)
    got[7] = send(after(piece[7], got[1]), 7)
    got[6] = send(after(piece[6], got[4]), 6)
    first = half(got, FIRST, (4, 5, 1, 0))
    first_far = far(first)
    second = half(got, SECOND, (3, 2, 7, 6))
    second_far = far(second)
    wholes = (root_left, root_right, stat_left, stat_right)
    left, right, stat_left, stat_right, z, x, block = stage(owner, z, x, wholes, count, first, second)
    own = join(first, second, z)
    right_sibling = sibling(right)
    own_sibling = sibling(own)
    first_both, second_both = sibling(first_far), sibling(second_far)
    right_both = sibling(right_far)
    blocks = [own, own_sibling, join(first_far, second_far), join(first_both, second_both)]
    rights = [right, right_sibling, right_far, right_both]
    product, sums = precondition(left, blocks, rights)
    sums = [sums] + [swap(sums, "rep", members, j) for j in (1, 2, 3)]
    left_new = statistic(stat_left, blocks, True)
    piece = rescale(product, sums, entries, count, left_new)
    back = {0: piece[0]}
    for d in (4, 1, 5, 6, 7, 3, 2):
        back[d] = send(piece[d], d)
    new = None
    for distances in ((4, 1, 5, 0), (6, 3), (7, 2)):
        new = update(block, z, x, back, distances, new)
    return (*new, left_new, statistic(stat_right, blocks, False))


def any_shape(flat, z, x, owner, stat_left, stat_right, root_left, root_right, count, members):
    q, width = root_left.shape
    entries = float(width**2)
    rows = flat.shape[0]
    sent = jnp.take(flat.reshape(rows, count, width), jnp.argsort(owner), axis=1)
    sent = sent.transpose(1, 0, 2).astype(BF16)
    own = lax.all_to_all(sent, "fsdp", 0, 0, tiled=True).reshape(q, width)
    blocks = gather_members(own, members)
    rights = gather_members(root_right, members)
    product, sums = precondition(root_left, blocks, rights)
    total = sum([sums] + [swap(sums, "rep", members, j) for j in range(1, members)]) / entries
    scale = jnp.sqrt(total[1, 0]) * lax.rsqrt(total[0, 0] + 1e-06)
    back = (scale * product).astype(BF16).reshape(count, rows, width)
    back = lax.all_to_all(back, "fsdp", 0, 0, tiled=True)
    back = jnp.take(back, owner, axis=0).transpose(1, 0, 2).reshape(z.shape).astype(F32)
    z_new = z - 0.2 * back
    x_new = 0.75 * x + 0.25 * z_new
    y_new = (0.1 * z_new + 0.9 * x_new).astype(BF16)
    return (z_new, x_new, y_new, statistic(stat_left, blocks, True), statistic(stat_right, blocks, False))


def per_device(grad, z_params, x_params, owner, stat_left, stat_right, root_left, root_right):
    count = lax.axis_size("fsdp")
    members = lax.axis_size("rep")
    plan = eight_by_four if (count, members) == (8, 4) else any_shape
    held = (stat_left[0], stat_right[0], root_left[0], root_right[0])
    new = plan(grad[0], z_params[0], x_params[0], owner, *held, count, members)
    return tuple(part[None] for part in new)


def solution(mesh):
    flat = P("rep", "fsdp", None)
    held = P("fsdp", "rep", None)
    return jax.shard_map(
        per_device,
        mesh=mesh,
        in_specs=(flat, flat, flat, P(), held, held, held, held),
        out_specs=(flat, flat, flat, held, held),
        check_vma=False,
    )
```

```python
import functools

import jax
import jax.numpy as jnp
from jax import lax
from jax.experimental import pallas as pl
from jax.experimental.pallas import tpu as pltpu
from jax.sharding import PartitionSpec as P

F32 = jnp.float32
BF16 = jnp.bfloat16
ANY = pl.BlockSpec(memory_space=pl.ANY)
VMEM = pl.BlockSpec(memory_space=pltpu.VMEM)
HBM = pl.BlockSpec(memory_space=pltpu.HBM)
MIB = 1 << 20


def params(mib):
    return pltpu.CompilerParams(vmem_limit_bytes=mib * MIB)


def cost(flops, moved):
    return pl.CostEstimate(flops=flops, bytes_accessed=moved, transcendentals=0)


def swap(x, axis, size, bit):
    return lax.ppermute(x, axis, [(i, i ^ bit) for i in range(size)])


def in_hbm(x):
    return pltpu.with_memory_space_constraint(x, pltpu.HBM)


def invert(owner_mem, block_mem, count):
    for b in range(count):
        block_mem[owner_mem[b]] = jnp.int32(b)


def route_kernel(owner_ref, grad_ref, *refs):
    outs, (owner_mem, block_mem, held, sems) = refs[:-4], refs[-4:]
    me = lax.axis_index("fsdp")
    count, rows, width = held.shape

    def load(b):
        start = b * width if isinstance(b, int) else pl.multiple_of(b * width, width)
        return pltpu.make_async_copy(
            grad_ref.at[:, pl.ds(start, width)], held.at[b], sems.at[b]
        )

    index = pltpu.make_async_copy(owner_ref, owner_mem, sems.at[count])
    index.start()
    for b in range(count):
        load(b).start()
    index.wait()
    invert(owner_mem, block_mem, count)
    for d in reversed(range(count)):
        b = block_mem[me ^ d]
        load(b).wait()
        outs[d][...] = held[b].astype(BF16)


def route(grad, owner, count):
    rows, width = grad.shape[0], grad.shape[1] // count
    return pl.pallas_call(
        route_kernel,
        out_shape=[jax.ShapeDtypeStruct((rows, width), BF16)] * count,
        in_specs=[HBM, HBM],
        out_specs=[VMEM] * count,
        scratch_shapes=[
            pltpu.SMEM((count,), jnp.int32),
            pltpu.SMEM((count,), jnp.int32),
            pltpu.VMEM((count, rows, width), F32),
            pltpu.SemaphoreType.DMA((count + 1,)),
        ],
        compiler_params=params(8),
        cost_estimate=cost(0, 6 * grad.size),
        name="route",
    )(in_hbm(owner), in_hbm(grad))


def local_call(kernel, shape, operands, name, *early):
    return pl.pallas_call(
        kernel,
        out_shape=jax.ShapeDtypeStruct(shape, BF16),
        in_specs=[VMEM] * len(operands) + [ANY] * len(early),
        out_specs=VMEM,
        compiler_params=params(8),
        cost_estimate=cost(0, 4 * shape[0] * shape[1]),
        name=name,
    )(*operands, *early)


FIRST = (0, 1, 4, 5)
SECOND = (2, 3, 6, 7)


def half_kernel(half_of, there, *refs):
    out_ref = refs[-1]
    rows = refs[0].shape[0]
    odd = lax.axis_index("fsdp") % 2
    for ref, d in zip(refs, there):
        place = half_of.index(d) // 2 * 2 + (odd ^ (d % 2))
        out_ref[pl.ds(pl.multiple_of(place * rows, rows), rows), :] = ref[...]


def half(got, half_of, there, *early):
    rows, width = got[0].shape
    kernel = functools.partial(half_kernel, half_of, there)
    return local_call(kernel, (4 * rows, width), [got[d] for d in there], "half", *early)


def join_kernel(first_ref, second_ref, *refs):
    out_ref = refs[-1]
    rows = first_ref.shape[0] // 2
    pair = lax.axis_index("fsdp") // 2
    for ref, half_of in ((first_ref, FIRST), (second_ref, SECOND)):
        for k in range(2):
            place = pl.multiple_of((pair ^ (half_of[2 * k] // 2)) * rows, rows)
            out_ref[pl.ds(place, rows), :] = ref[k * rows : (k + 1) * rows, :]


def join(first, second, *early):
    shape = (2 * first.shape[0], first.shape[1])
    return local_call(join_kernel, shape, (first, second), "join", *early)


def after(x, first):
    def kernel(x_ref, first_ref, out_ref):
        pass

    return pl.pallas_call(
        kernel,
        out_shape=jax.ShapeDtypeStruct(x.shape, x.dtype),
        in_specs=[ANY, ANY],
        out_specs=ANY,
        input_output_aliases={0: 0},
        compiler_params=params(1),
        cost_estimate=cost(0, 0),
        name="after",
    )(x, first)


def precond_kernel(members, left_ref, *refs):
    g_refs, r_refs = refs[:members], refs[members : 2 * members]
    out_ref, sums_ref, mid_ref = refs[-3:]
    member = lax.axis_index("rep")
    q = left_ref.shape[0]

    def part(ref, j):
        return ref[:, pl.ds(pl.multiple_of((member ^ j) * q, q), q)]

    def chain(ref, rights):
        total = jnp.dot(part(ref, 0), rights[0][...], preferred_element_type=F32)
        for j in range(1, members):
            total += jnp.dot(part(ref, j), rights[j][...], preferred_element_type=F32)
        return total

    mid_ref[...] = chain(left_ref, g_refs).astype(BF16)
    product = chain(mid_ref, r_refs)
    out_ref[...] = product
    own = g_refs[0][...].astype(F32)
    rows = lax.broadcasted_iota(jnp.int32, sums_ref.shape, 0)
    sums_ref[...] = jnp.where(rows == 0, jnp.sum(product * product), jnp.sum(own * own))


def precondition(left, blocks, rights, *early):
    q, width = left.shape
    members = len(blocks)
    return pl.pallas_call(
        functools.partial(precond_kernel, members),
        out_shape=[
            jax.ShapeDtypeStruct((q, width), F32),
            jax.ShapeDtypeStruct((8, 128), F32),
        ],
        in_specs=[VMEM] * (1 + 2 * members) + [ANY] * len(early),
        out_specs=[VMEM, VMEM],
        scratch_shapes=[pltpu.VMEM((q, width), BF16)],
        compiler_params=params(16),
        cost_estimate=cost(4 * q * width * width, 4 * width * width + 4 * q * width),
        name="precondition",
    )(left, *blocks, *rights, *early)


def scale_kernel(entries, count, n, product_ref, *refs):
    sums_refs, outs = refs[:n], refs[-count:]
    me = lax.axis_index("fsdp")
    rows = outs[0].shape[0]
    total = sum(ref[...] for ref in sums_refs) / entries
    scale = jnp.sqrt(total[1:2, :1]) * lax.rsqrt(total[:1, :1] + 1e-06)
    for d, out_ref in enumerate(outs):
        part = product_ref[pl.ds(pl.multiple_of((me ^ d) * rows, rows), rows), :]
        out_ref[...] = (scale * part).astype(BF16)


def rescale(product, sums, entries, count, *early):
    rows, width = product.shape[0] // count, product.shape[1]
    return pl.pallas_call(
        functools.partial(scale_kernel, entries, count, len(sums)),
        out_shape=[jax.ShapeDtypeStruct((rows, width), BF16)] * count,
        in_specs=[VMEM] * (1 + len(sums)) + [HBM] * len(early),
        out_specs=[VMEM] * count,
        compiler_params=params(8),
        cost_estimate=cost(product.size, 6 * product.size),
        name="rescale",
    )(product, *sums, *map(in_hbm, early))


def stats_kernel(members, rows_side, old_ref, *refs):
    g_refs = refs[:members]
    new_out, new_mem, sems = refs[members:]
    member = lax.axis_index("rep")
    q, width = old_ref.shape
    step = 0.05 / width
    strip = pl.ds(pl.multiple_of(member * q, q), q)
    stores = []
    for j in range(members):
        if rows_side:
            cols = pl.ds(pl.multiple_of((member ^ j) * q, q), q)
            product = lax.dot_general(
                g_refs[0][...], g_refs[j][...], (((1,), (1,)), ((), ())), preferred_element_type=F32
            )
        else:
            cols = pl.ds(j * q, q)
            product = sum(
                lax.dot_general(
                    g[:, strip], g[:, cols], (((0,), (0,)), ((), ())), preferred_element_type=F32
                )
                for g in g_refs
            )
        new_mem[j] = 0.95 * old_ref[:, cols] + step * product
        stores.append(pltpu.make_async_copy(new_mem.at[j], new_out.at[:, cols], sems.at[j]))
        stores[-1].start()
    for store in stores:
        store.wait()


def statistic(old, blocks, rows_side):
    q, width = old.shape
    members = len(blocks)
    return pl.pallas_call(
        functools.partial(stats_kernel, members, rows_side),
        out_shape=jax.ShapeDtypeStruct((q, width), F32),
        in_specs=[VMEM] * (1 + members),
        out_specs=HBM,
        scratch_shapes=[
            pltpu.VMEM((members, q, q), F32),
            pltpu.SemaphoreType.DMA((members,)),
        ],
        compiler_params=params(16),
        cost_estimate=cost(2 * q * width * width, 8 * q * width + 2 * width * width),
        name="left_statistic" if rows_side else "right_statistic",
    )(old, *blocks)


def stage_kernel(n, owner_ref, z_ref, x_ref, *refs):
    whole_refs, whole_outs = refs[:n], refs[-n - 6 : -6]
    z_out, x_out, block_out, owner_mem, block_mem, sems = refs[-6:]
    me = lax.axis_index("fsdp")
    count, _, width = z_out.shape
    index = pltpu.make_async_copy(owner_ref, owner_mem, sems.at[2, n])
    index.start()
    loads = [
        pltpu.make_async_copy(src, dst, sems.at[2, i])
        for i, (src, dst) in enumerate(zip(whole_refs, whole_outs))
    ]
    for load in loads:
        load.start()
    index.wait()
    invert(owner_mem, block_mem, count)
    for d in range(count):
        block = block_mem[me ^ d]
        block_out[pl.ds(d, 1), :] = jnp.full((1, block_out.shape[1]), block, jnp.int32)
        cols = pl.ds(pl.multiple_of(block * width, width), width)
        for i, (src, dst) in enumerate(((z_ref, z_out), (x_ref, x_out))):
            load = pltpu.make_async_copy(src.at[:, cols], dst.at[d], sems.at[i, d])
            load.start()
            loads.append(load)
    for load in loads:
        load.wait()


def stage(owner, z, x, wholes, count, *early):
    rows, width = z.shape[0], z.shape[1] // count
    n = len(wholes)
    moved = sum(2 * w.size * w.dtype.itemsize for w in wholes)
    return pl.pallas_call(
        functools.partial(stage_kernel, n),
        out_shape=[jax.ShapeDtypeStruct(w.shape, w.dtype) for w in wholes]
        + [
            jax.ShapeDtypeStruct((count, rows, width), F32),
            jax.ShapeDtypeStruct((count, rows, width), F32),
            jax.ShapeDtypeStruct((count, 128), jnp.int32),
        ],
        in_specs=[HBM] * (3 + n) + [ANY] * len(early),
        out_specs=[VMEM] * (n + 3),
        scratch_shapes=[
            pltpu.SMEM((count,), jnp.int32),
            pltpu.SMEM((count,), jnp.int32),
            pltpu.SemaphoreType.DMA((3, count)),
        ],
        compiler_params=params(8),
        cost_estimate=cost(0, 16 * z.size + moved),
        name="stage",
    )(*[in_hbm(a) for a in (owner, z, x, *wholes)], *early)


def update_kernel(distances, fresh, block_ref, z_ref, x_ref, *refs):
    n = len(distances)
    back, outs = refs[:n], refs[n : n + 3] if fresh else refs[n + 3 : n + 6]
    z_mem, x_mem, y_mem, sems = refs[-4:]
    width = z_ref.shape[2]
    blocks = [block_ref[d, 0] for d in distances]
    stores = []
    for k, d in enumerate(distances):
        z_new = z_ref[d] - 0.2 * back[k][...].astype(F32)
        x_new = 0.75 * x_ref[d] + 0.25 * z_new
        z_mem[k] = z_new
        x_mem[k] = x_new
        y_mem[k] = (0.1 * z_new + 0.9 * x_new).astype(BF16)
        cols = pl.ds(pl.multiple_of(blocks[k] * width, width), width)
        for i, mem in enumerate((z_mem, x_mem, y_mem)):
            store = pltpu.make_async_copy(mem.at[k], outs[i].at[:, cols], sems.at[i, k])
            store.start()
            stores.append(store)
    for store in stores:
        store.wait()


def update(block, z, x, back, distances, held=None):
    count, rows, width = z.shape
    flat = (rows, count * width)
    n = len(distances)
    fresh = held is None
    return pl.pallas_call(
        functools.partial(update_kernel, distances, fresh),
        out_shape=[
            jax.ShapeDtypeStruct(flat, F32),
            jax.ShapeDtypeStruct(flat, F32),
            jax.ShapeDtypeStruct(flat, BF16),
        ],
        in_specs=[VMEM] * (3 + n) + ([] if fresh else [HBM] * 3),
        out_specs=[HBM] * 3,
        input_output_aliases={} if fresh else {3 + n + i: i for i in range(3)},
        scratch_shapes=[
            pltpu.VMEM((n, rows, width), F32),
            pltpu.VMEM((n, rows, width), F32),
            pltpu.VMEM((n, rows, width), BF16),
            pltpu.SemaphoreType.DMA((3, n)),
        ],
        compiler_params=params(16),
        cost_estimate=cost(8 * n * rows * width, 20 * n * rows * width),
        name="update",
    )(block, z, x, *[back[d] for d in distances], *([] if fresh else held))


def gather_members(own, members):
    bit = members // 2
    got = {0: own}
    while bit:
        for known in list(got):
            got[known ^ bit] = swap(got[known], "rep", members, bit)
        bit //= 2
    return [got[j] for j in range(members)]


def eight_by_four(flat, z, x, owner, stat_left, stat_right, root_left, root_right, count, members):
    def send(piece, d):
        return swap(piece, "fsdp", count, d)

    def far(piece):
        return swap(piece, "rep", members, 2)

    def sibling(piece):
        return swap(piece, "rep", members, 1)

    entries = float(stat_left.shape[1] ** 2)
    right_far = far(root_right)
    piece = route(flat, owner, count)
    got = {0: piece[0]}
    for d in (4, 5, 3, 1):
        got[d] = send(piece[d], d)
    got[2] = send(after(piece[2], got[3]), 2)
    got[7] = send(after(piece[7], got[1]), 7)
    got[6] = send(after(piece[6], got[4]), 6)
    first = half(got, FIRST, (4, 5, 1, 0))
    first_far = far(first)
    second = half(got, SECOND, (3, 2, 7, 6))
    second_far = far(second)
    wholes = (root_left, root_right, stat_left, stat_right)
    left, right, stat_left, stat_right, z, x, block = stage(owner, z, x, wholes, count, first, second)
    own = join(first, second, z)
    right_sibling = sibling(right)
    own_sibling = sibling(own)
    first_both, second_both = sibling(first_far), sibling(second_far)
    right_both = sibling(right_far)
    blocks = [own, own_sibling, join(first_far, second_far), join(first_both, second_both)]
    rights = [right, right_sibling, right_far, right_both]
    product, sums = precondition(left, blocks, rights)
    sums = [sums] + [swap(sums, "rep", members, j) for j in (1, 2, 3)]
    left_new = statistic(stat_left, blocks, True)
    piece = rescale(product, sums, entries, count, left_new)
    back = {0: piece[0]}
    for d in (4, 1, 5, 6, 7, 3, 2):
        back[d] = send(piece[d], d)
    new = None
    for distances in ((4, 1, 5, 6, 0), (7, 3, 2)):
        new = update(block, z, x, back, distances, new)
    return (*new, left_new, statistic(stat_right, blocks, False))


def any_shape(flat, z, x, owner, stat_left, stat_right, root_left, root_right, count, members):
    q, width = root_left.shape
    entries = float(width**2)
    rows = flat.shape[0]
    sent = jnp.take(flat.reshape(rows, count, width), jnp.argsort(owner), axis=1)
    sent = sent.transpose(1, 0, 2).astype(BF16)
    own = lax.all_to_all(sent, "fsdp", 0, 0, tiled=True).reshape(q, width)
    blocks = gather_members(own, members)
    rights = gather_members(root_right, members)
    product, sums = precondition(root_left, blocks, rights)
    total = sum([sums] + [swap(sums, "rep", members, j) for j in range(1, members)]) / entries
    scale = jnp.sqrt(total[1, 0]) * lax.rsqrt(total[0, 0] + 1e-06)
    back = (scale * product).astype(BF16).reshape(count, rows, width)
    back = lax.all_to_all(back, "fsdp", 0, 0, tiled=True)
    back = jnp.take(back, owner, axis=0).transpose(1, 0, 2).reshape(z.shape).astype(F32)
    z_new = z - 0.2 * back
    x_new = 0.75 * x + 0.25 * z_new
    y_new = (0.1 * z_new + 0.9 * x_new).astype(BF16)
    return (z_new, x_new, y_new, statistic(stat_left, blocks, True), statistic(stat_right, blocks, False))


def per_device(grad, z_params, x_params, owner, stat_left, stat_right, root_left, root_right):
    count = lax.axis_size("fsdp")
    members = lax.axis_size("rep")
    plan = eight_by_four if (count, members) == (8, 4) else any_shape
    held = (stat_left[0], stat_right[0], root_left[0], root_right[0])
    new = plan(grad[0], z_params[0], x_params[0], owner, *held, count, members)
    return tuple(part[None] for part in new)


def solution(mesh):
    flat = P("rep", "fsdp", None)
    held = P("fsdp", "rep", None)
    return jax.shard_map(
        per_device,
        mesh=mesh,
        in_specs=(flat, flat, flat, P(), held, held, held, held),
        out_specs=(flat, flat, flat, held, held),
        check_vma=False,
    )
```

```python
import functools

import jax
import jax.numpy as jnp
from jax import lax
from jax.experimental import pallas as pl
from jax.experimental.pallas import tpu as pltpu
from jax.sharding import PartitionSpec as P

F32 = jnp.float32
BF16 = jnp.bfloat16
ANY = pl.BlockSpec(memory_space=pl.ANY)
VMEM = pl.BlockSpec(memory_space=pltpu.VMEM)
HBM = pl.BlockSpec(memory_space=pltpu.HBM)
MIB = 1 << 20


def params(mib):
    return pltpu.CompilerParams(vmem_limit_bytes=mib * MIB)


def cost(flops, moved):
    return pl.CostEstimate(flops=flops, bytes_accessed=moved, transcendentals=0)


def swap(x, axis, size, bit):
    return lax.ppermute(x, axis, [(i, i ^ bit) for i in range(size)])


def in_hbm(x):
    return pltpu.with_memory_space_constraint(x, pltpu.HBM)


def invert(owner_mem, block_mem, count):
    for b in range(count):
        block_mem[owner_mem[b]] = jnp.int32(b)


def route_kernel(owner_ref, grad_ref, *refs):
    outs, (owner_mem, block_mem, held, sems) = refs[:-4], refs[-4:]
    me = lax.axis_index("fsdp")
    count, rows, width = held.shape

    def load(b):
        start = b * width if isinstance(b, int) else pl.multiple_of(b * width, width)
        return pltpu.make_async_copy(
            grad_ref.at[:, pl.ds(start, width)], held.at[b], sems.at[b]
        )

    index = pltpu.make_async_copy(owner_ref, owner_mem, sems.at[count])
    index.start()
    for b in range(count):
        load(b).start()
    index.wait()
    invert(owner_mem, block_mem, count)
    for d in reversed(range(count)):
        b = block_mem[me ^ d]
        load(b).wait()
        outs[d][...] = held[b].astype(BF16)


def route(grad, owner, count):
    rows, width = grad.shape[0], grad.shape[1] // count
    return pl.pallas_call(
        route_kernel,
        out_shape=[jax.ShapeDtypeStruct((rows, width), BF16)] * count,
        in_specs=[HBM, HBM],
        out_specs=[VMEM] * count,
        scratch_shapes=[
            pltpu.SMEM((count,), jnp.int32),
            pltpu.SMEM((count,), jnp.int32),
            pltpu.VMEM((count, rows, width), F32),
            pltpu.SemaphoreType.DMA((count + 1,)),
        ],
        compiler_params=params(8),
        cost_estimate=cost(0, 6 * grad.size),
        name="route",
    )(in_hbm(owner), in_hbm(grad))


def local_call(kernel, shape, operands, name, *early):
    return pl.pallas_call(
        kernel,
        out_shape=jax.ShapeDtypeStruct(shape, BF16),
        in_specs=[VMEM] * len(operands) + [ANY] * len(early),
        out_specs=VMEM,
        compiler_params=params(8),
        cost_estimate=cost(0, 4 * shape[0] * shape[1]),
        name=name,
    )(*operands, *early)


FIRST = (0, 1, 4, 5)
SECOND = (2, 3, 6, 7)


def half_kernel(half_of, there, *refs):
    out_ref = refs[-1]
    rows = refs[0].shape[0]
    odd = lax.axis_index("fsdp") % 2
    for ref, d in zip(refs, there):
        place = half_of.index(d) // 2 * 2 + (odd ^ (d % 2))
        out_ref[pl.ds(pl.multiple_of(place * rows, rows), rows), :] = ref[...]


def half(got, half_of, there, *early):
    rows, width = got[0].shape
    kernel = functools.partial(half_kernel, half_of, there)
    return local_call(kernel, (4 * rows, width), [got[d] for d in there], "half", *early)


def join_kernel(first_ref, second_ref, *refs):
    out_ref = refs[-1]
    rows = first_ref.shape[0] // 2
    pair = lax.axis_index("fsdp") // 2
    for ref, half_of in ((first_ref, FIRST), (second_ref, SECOND)):
        for k in range(2):
            place = pl.multiple_of((pair ^ (half_of[2 * k] // 2)) * rows, rows)
            out_ref[pl.ds(place, rows), :] = ref[k * rows : (k + 1) * rows, :]


def join(first, second, *early):
    shape = (2 * first.shape[0], first.shape[1])
    return local_call(join_kernel, shape, (first, second), "join", *early)


def after(x, first):
    def kernel(x_ref, first_ref, out_ref):
        pass

    return pl.pallas_call(
        kernel,
        out_shape=jax.ShapeDtypeStruct(x.shape, x.dtype),
        in_specs=[ANY, ANY],
        out_specs=ANY,
        input_output_aliases={0: 0},
        compiler_params=params(1),
        cost_estimate=cost(0, 0),
        name="after",
    )(x, first)


def precond_kernel(members, left_ref, *refs):
    g_refs, r_refs = refs[:members], refs[members : 2 * members]
    out_ref, sums_ref, mid_ref = refs[-3:]
    member = lax.axis_index("rep")
    q = left_ref.shape[0]

    def part(ref, j):
        return ref[:, pl.ds(pl.multiple_of((member ^ j) * q, q), q)]

    def chain(ref, rights):
        total = jnp.dot(part(ref, 0), rights[0][...], preferred_element_type=F32)
        for j in range(1, members):
            total += jnp.dot(part(ref, j), rights[j][...], preferred_element_type=F32)
        return total

    mid_ref[...] = chain(left_ref, g_refs).astype(BF16)
    product = chain(mid_ref, r_refs)
    out_ref[...] = product
    own = g_refs[0][...].astype(F32)
    rows = lax.broadcasted_iota(jnp.int32, sums_ref.shape, 0)
    sums_ref[...] = jnp.where(rows == 0, jnp.sum(product * product), jnp.sum(own * own))


def precondition(left, blocks, rights, *early):
    q, width = left.shape
    members = len(blocks)
    return pl.pallas_call(
        functools.partial(precond_kernel, members),
        out_shape=[
            jax.ShapeDtypeStruct((q, width), F32),
            jax.ShapeDtypeStruct((8, 128), F32),
        ],
        in_specs=[VMEM] * (1 + 2 * members) + [ANY] * len(early),
        out_specs=[VMEM, VMEM],
        scratch_shapes=[pltpu.VMEM((q, width), BF16)],
        compiler_params=params(16),
        cost_estimate=cost(4 * q * width * width, 4 * width * width + 4 * q * width),
        name="precondition",
    )(left, *blocks, *rights, *early)


def scale_kernel(entries, count, n, product_ref, *refs):
    sums_refs, outs = refs[:n], refs[-count:]
    me = lax.axis_index("fsdp")
    rows = outs[0].shape[0]
    total = sum(ref[...] for ref in sums_refs) / entries
    scale = jnp.sqrt(total[1:2, :1]) * lax.rsqrt(total[:1, :1] + 1e-06)
    for d, out_ref in enumerate(outs):
        part = product_ref[pl.ds(pl.multiple_of((me ^ d) * rows, rows), rows), :]
        out_ref[...] = (scale * part).astype(BF16)


def rescale(product, sums, entries, count, *early):
    rows, width = product.shape[0] // count, product.shape[1]
    return pl.pallas_call(
        functools.partial(scale_kernel, entries, count, len(sums)),
        out_shape=[jax.ShapeDtypeStruct((rows, width), BF16)] * count,
        in_specs=[VMEM] * (1 + len(sums)) + [HBM] * len(early),
        out_specs=[VMEM] * count,
        compiler_params=params(8),
        cost_estimate=cost(product.size, 6 * product.size),
        name="rescale",
    )(product, *sums, *map(in_hbm, early))


def start_statistic(rows_side, old_ref, g_refs, new_out, new_mem, sems):
    members = len(g_refs)
    member = lax.axis_index("rep")
    q, width = old_ref.shape
    step = 0.05 / width
    strip = pl.ds(pl.multiple_of(member * q, q), q)
    stores = []
    for j in range(members):
        if rows_side:
            cols = pl.ds(pl.multiple_of((member ^ j) * q, q), q)
            product = lax.dot_general(
                g_refs[0][...], g_refs[j][...], (((1,), (1,)), ((), ())), preferred_element_type=F32
            )
        else:
            cols = pl.ds(j * q, q)
            product = sum(
                lax.dot_general(
                    g[:, strip], g[:, cols], (((0,), (0,)), ((), ())), preferred_element_type=F32
                )
                for g in g_refs
            )
        new_mem[j] = 0.95 * old_ref[:, cols] + step * product
        stores.append(pltpu.make_async_copy(new_mem.at[j], new_out.at[:, cols], sems.at[j]))
        stores[-1].start()
    return stores


def stats_kernel(members, rows_side, old_ref, *refs):
    for store in start_statistic(rows_side, old_ref, refs[:members], *refs[members:]):
        store.wait()


def statistic(old, blocks, rows_side):
    q, width = old.shape
    members = len(blocks)
    return pl.pallas_call(
        functools.partial(stats_kernel, members, rows_side),
        out_shape=jax.ShapeDtypeStruct((q, width), F32),
        in_specs=[VMEM] * (1 + members),
        out_specs=HBM,
        scratch_shapes=[
            pltpu.VMEM((members, q, q), F32),
            pltpu.SemaphoreType.DMA((members,)),
        ],
        compiler_params=params(16),
        cost_estimate=cost(2 * q * width * width, 8 * q * width + 2 * width * width),
        name="left_statistic" if rows_side else "right_statistic",
    )(old, *blocks)


def stage_kernel(n, owner_ref, z_ref, x_ref, *refs):
    whole_refs, whole_outs = refs[:n], refs[-n - 6 : -6]
    z_out, x_out, block_out, owner_mem, block_mem, sems = refs[-6:]
    me = lax.axis_index("fsdp")
    count, _, width = z_out.shape
    index = pltpu.make_async_copy(owner_ref, owner_mem, sems.at[2, n])
    index.start()
    loads = [
        pltpu.make_async_copy(src, dst, sems.at[2, i])
        for i, (src, dst) in enumerate(zip(whole_refs, whole_outs))
    ]
    for load in loads:
        load.start()
    index.wait()
    invert(owner_mem, block_mem, count)
    for d in range(count):
        block = block_mem[me ^ d]
        block_out[pl.ds(d, 1), :] = jnp.full((1, block_out.shape[1]), block, jnp.int32)
        cols = pl.ds(pl.multiple_of(block * width, width), width)
        for i, (src, dst) in enumerate(((z_ref, z_out), (x_ref, x_out))):
            load = pltpu.make_async_copy(src.at[:, cols], dst.at[d], sems.at[i, d])
            load.start()
            loads.append(load)
    for load in loads:
        load.wait()


def stage(owner, z, x, wholes, count, *early):
    rows, width = z.shape[0], z.shape[1] // count
    n = len(wholes)
    moved = sum(2 * w.size * w.dtype.itemsize for w in wholes)
    return pl.pallas_call(
        functools.partial(stage_kernel, n),
        out_shape=[jax.ShapeDtypeStruct(w.shape, w.dtype) for w in wholes]
        + [
            jax.ShapeDtypeStruct((count, rows, width), F32),
            jax.ShapeDtypeStruct((count, rows, width), F32),
            jax.ShapeDtypeStruct((count, 128), jnp.int32),
        ],
        in_specs=[HBM] * (3 + n) + [ANY] * len(early),
        out_specs=[VMEM] * (n + 3),
        scratch_shapes=[
            pltpu.SMEM((count,), jnp.int32),
            pltpu.SMEM((count,), jnp.int32),
            pltpu.SemaphoreType.DMA((3, count)),
        ],
        compiler_params=params(8),
        cost_estimate=cost(0, 16 * z.size + moved),
        name="stage",
    )(*[in_hbm(a) for a in (owner, z, x, *wholes)], *early)


def update_kernel(distances, members, block_ref, z_ref, x_ref, *refs):
    n = len(distances)
    back, refs = refs[:n], refs[n:]
    stores = []
    if members:
        outs, (z_mem, x_mem, y_mem, sems) = refs[members + 1 : members + 4], refs[-6:-2]
        new_out = refs[members + 4]
        stores += start_statistic(False, refs[0], refs[1 : members + 1], new_out, *refs[-2:])
    else:
        outs, (z_mem, x_mem, y_mem, sems) = refs[3:6], refs[-4:]
    width = z_ref.shape[2]
    blocks = [block_ref[d, 0] for d in distances]
    for k, d in enumerate(distances):
        z_new = z_ref[d] - 0.2 * back[k][...].astype(F32)
        x_new = 0.75 * x_ref[d] + 0.25 * z_new
        z_mem[k] = z_new
        x_mem[k] = x_new
        y_mem[k] = (0.1 * z_new + 0.9 * x_new).astype(BF16)
        cols = pl.ds(pl.multiple_of(blocks[k] * width, width), width)
        for i, mem in enumerate((z_mem, x_mem, y_mem)):
            store = pltpu.make_async_copy(mem.at[k], outs[i].at[:, cols], sems.at[i, k])
            store.start()
            stores.append(store)
    for store in stores:
        store.wait()


def update(block, z, x, back, distances, held=None, stat=()):
    count, rows, width = z.shape
    flat = (rows, count * width)
    n = len(distances)
    fresh = held is None
    extra = []
    if stat:
        members, q = len(stat) - 1, stat[0].shape[0]
        extra = [pltpu.VMEM((members, q, q), F32), pltpu.SemaphoreType.DMA((members,))]
    return pl.pallas_call(
        functools.partial(update_kernel, distances, len(stat[1:])),
        out_shape=[
            jax.ShapeDtypeStruct(flat, F32),
            jax.ShapeDtypeStruct(flat, F32),
            jax.ShapeDtypeStruct(flat, BF16),
        ]
        + [jax.ShapeDtypeStruct(old.shape, F32) for old in stat[:1]],
        in_specs=[VMEM] * (3 + n) + [VMEM] * len(stat) + ([] if fresh else [HBM] * 3),
        out_specs=[HBM] * (4 if stat else 3),
        input_output_aliases={} if fresh else {3 + n + i: i for i in range(3)},
        scratch_shapes=[
            pltpu.VMEM((n, rows, width), F32),
            pltpu.VMEM((n, rows, width), F32),
            pltpu.VMEM((n, rows, width), BF16),
            pltpu.SemaphoreType.DMA((3, n)),
        ]
        + extra,
        compiler_params=params(16),
        cost_estimate=cost(8 * n * rows * width, 20 * n * rows * width),
        name="update",
    )(block, z, x, *[back[d] for d in distances], *stat, *([] if fresh else held))


def gather_members(own, members):
    bit = members // 2
    got = {0: own}
    while bit:
        for known in list(got):
            got[known ^ bit] = swap(got[known], "rep", members, bit)
        bit //= 2
    return [got[j] for j in range(members)]


def eight_by_four(flat, z, x, owner, stat_left, stat_right, root_left, root_right, count, members):
    def send(piece, d):
        return swap(piece, "fsdp", count, d)

    def far(piece):
        return swap(piece, "rep", members, 2)

    def sibling(piece):
        return swap(piece, "rep", members, 1)

    entries = float(stat_left.shape[1] ** 2)
    right_far = far(root_right)
    piece = route(flat, owner, count)
    got = {0: piece[0]}
    for d in (4, 5, 3, 1):
        got[d] = send(piece[d], d)
    got[2] = send(after(piece[2], got[3]), 2)
    got[7] = send(after(piece[7], got[1]), 7)
    got[6] = send(after(piece[6], got[4]), 6)
    first = half(got, FIRST, (4, 5, 1, 0))
    first_far = far(first)
    second = half(got, SECOND, (3, 2, 7, 6))
    second_far = far(second)
    wholes = (root_left, root_right, stat_left, stat_right)
    left, right, stat_left, stat_right, z, x, block = stage(owner, z, x, wholes, count, first, second)
    own = join(first, second, z)
    right_sibling = sibling(right)
    own_sibling = sibling(own)
    first_both, second_both = sibling(first_far), sibling(second_far)
    right_both = sibling(right_far)
    blocks = [own, own_sibling, join(first_far, second_far), join(first_both, second_both)]
    rights = [right, right_sibling, right_far, right_both]
    product, sums = precondition(left, blocks, rights)
    sums = [sums] + [swap(sums, "rep", members, j) for j in (1, 2, 3)]
    left_new = statistic(stat_left, blocks, True)
    piece = rescale(product, sums, entries, count, left_new)
    back = {0: piece[0]}
    for d in (4, 1, 5, 6, 7, 3, 2):
        back[d] = send(piece[d], d)
    *new, right_new = update(block, z, x, back, (4, 1, 5, 6, 0), None, (stat_right, *blocks))
    new = update(block, z, x, back, (7, 3, 2), new)
    return (*new, left_new, right_new)


def any_shape(flat, z, x, owner, stat_left, stat_right, root_left, root_right, count, members):
    q, width = root_left.shape
    entries = float(width**2)
    rows = flat.shape[0]
    sent = jnp.take(flat.reshape(rows, count, width), jnp.argsort(owner), axis=1)
    sent = sent.transpose(1, 0, 2).astype(BF16)
    own = lax.all_to_all(sent, "fsdp", 0, 0, tiled=True).reshape(q, width)
    blocks = gather_members(own, members)
    rights = gather_members(root_right, members)
    product, sums = precondition(root_left, blocks, rights)
    total = sum([sums] + [swap(sums, "rep", members, j) for j in range(1, members)]) / entries
    scale = jnp.sqrt(total[1, 0]) * lax.rsqrt(total[0, 0] + 1e-06)
    back = (scale * product).astype(BF16).reshape(count, rows, width)
    back = lax.all_to_all(back, "fsdp", 0, 0, tiled=True)
    back = jnp.take(back, owner, axis=0).transpose(1, 0, 2).reshape(z.shape).astype(F32)
    z_new = z - 0.2 * back
    x_new = 0.75 * x + 0.25 * z_new
    y_new = (0.1 * z_new + 0.9 * x_new).astype(BF16)
    return (z_new, x_new, y_new, statistic(stat_left, blocks, True), statistic(stat_right, blocks, False))


def per_device(grad, z_params, x_params, owner, stat_left, stat_right, root_left, root_right):
    count = lax.axis_size("fsdp")
    members = lax.axis_size("rep")
    plan = eight_by_four if (count, members) == (8, 4) else any_shape
    held = (stat_left[0], stat_right[0], root_left[0], root_right[0])
    new = plan(grad[0], z_params[0], x_params[0], owner, *held, count, members)
    return tuple(part[None] for part in new)


def solution(mesh):
    flat = P("rep", "fsdp", None)
    held = P("fsdp", "rep", None)
    return jax.shard_map(
        per_device,
        mesh=mesh,
        in_specs=(flat, flat, flat, P(), held, held, held, held),
        out_specs=(flat, flat, flat, held, held),
        check_vma=False,
    )
```

```python
import functools

import jax
import jax.numpy as jnp
from jax import lax
from jax.experimental import pallas as pl
from jax.experimental.pallas import tpu as pltpu
from jax.sharding import PartitionSpec as P

F32 = jnp.float32
BF16 = jnp.bfloat16
ANY = pl.BlockSpec(memory_space=pl.ANY)
VMEM = pl.BlockSpec(memory_space=pltpu.VMEM)
HBM = pl.BlockSpec(memory_space=pltpu.HBM)
MIB = 1 << 20


def params(mib):
    return pltpu.CompilerParams(vmem_limit_bytes=mib * MIB)


def cost(flops, moved):
    return pl.CostEstimate(flops=flops, bytes_accessed=moved, transcendentals=0)


def swap(x, axis, size, bit):
    return lax.ppermute(x, axis, [(i, i ^ bit) for i in range(size)])


def in_hbm(x):
    return pltpu.with_memory_space_constraint(x, pltpu.HBM)


def invert(owner_mem, block_mem, count):
    for b in range(count):
        block_mem[owner_mem[b]] = jnp.int32(b)


def route_kernel(owner_ref, grad_ref, *refs):
    outs, (owner_mem, block_mem, held, sems) = refs[:-4], refs[-4:]
    me = lax.axis_index("fsdp")
    count, rows, width = held.shape

    def load(b):
        start = b * width if isinstance(b, int) else pl.multiple_of(b * width, width)
        return pltpu.make_async_copy(
            grad_ref.at[:, pl.ds(start, width)], held.at[b], sems.at[b]
        )

    index = pltpu.make_async_copy(owner_ref, owner_mem, sems.at[count])
    index.start()
    for b in range(count):
        load(b).start()
    index.wait()
    invert(owner_mem, block_mem, count)
    for d in reversed(range(count)):
        b = block_mem[me ^ d]
        load(b).wait()
        outs[d][...] = held[b].astype(BF16)


def route(grad, owner, count):
    rows, width = grad.shape[0], grad.shape[1] // count
    return pl.pallas_call(
        route_kernel,
        out_shape=[jax.ShapeDtypeStruct((rows, width), BF16)] * count,
        in_specs=[HBM, HBM],
        out_specs=[VMEM] * count,
        scratch_shapes=[
            pltpu.SMEM((count,), jnp.int32),
            pltpu.SMEM((count,), jnp.int32),
            pltpu.VMEM((count, rows, width), F32),
            pltpu.SemaphoreType.DMA((count + 1,)),
        ],
        compiler_params=params(8),
        cost_estimate=cost(0, 6 * grad.size),
        name="route",
    )(in_hbm(owner), in_hbm(grad))


def local_call(kernel, shape, operands, name, *early):
    return pl.pallas_call(
        kernel,
        out_shape=jax.ShapeDtypeStruct(shape, BF16),
        in_specs=[VMEM] * len(operands) + [ANY] * len(early),
        out_specs=VMEM,
        compiler_params=params(8),
        cost_estimate=cost(0, 4 * shape[0] * shape[1]),
        name=name,
    )(*operands, *early)


FIRST = (0, 1, 4, 5)
SECOND = (2, 3, 6, 7)


def half_kernel(half_of, there, *refs):
    out_ref = refs[-1]
    rows = refs[0].shape[0]
    odd = lax.axis_index("fsdp") % 2
    for ref, d in zip(refs, there):
        place = half_of.index(d) // 2 * 2 + (odd ^ (d % 2))
        out_ref[pl.ds(pl.multiple_of(place * rows, rows), rows), :] = ref[...]


def half(got, half_of, there, *early):
    rows, width = got[0].shape
    kernel = functools.partial(half_kernel, half_of, there)
    return local_call(kernel, (4 * rows, width), [got[d] for d in there], "half", *early)


def join_kernel(first_ref, second_ref, *refs):
    out_ref = refs[-1]
    rows = first_ref.shape[0] // 2
    pair = lax.axis_index("fsdp") // 2
    for ref, half_of in ((first_ref, FIRST), (second_ref, SECOND)):
        for k in range(2):
            place = pl.multiple_of((pair ^ (half_of[2 * k] // 2)) * rows, rows)
            out_ref[pl.ds(place, rows), :] = ref[k * rows : (k + 1) * rows, :]


def join(first, second, *early):
    shape = (2 * first.shape[0], first.shape[1])
    return local_call(join_kernel, shape, (first, second), "join", *early)


def after(x, first):
    def kernel(x_ref, first_ref, out_ref):
        pass

    return pl.pallas_call(
        kernel,
        out_shape=jax.ShapeDtypeStruct(x.shape, x.dtype),
        in_specs=[ANY, ANY],
        out_specs=ANY,
        input_output_aliases={0: 0},
        compiler_params=params(1),
        cost_estimate=cost(0, 0),
        name="after",
    )(x, first)


def precond_kernel(members, left_ref, *refs):
    g_refs, r_refs = refs[:members], refs[members : 2 * members]
    out_ref, sums_ref, mid_ref = refs[-3:]
    member = lax.axis_index("rep")
    q = left_ref.shape[0]

    def part(ref, j):
        return ref[:, pl.ds(pl.multiple_of((member ^ j) * q, q), q)]

    def chain(ref, rights):
        total = jnp.dot(part(ref, 0), rights[0][...], preferred_element_type=F32)
        for j in range(1, members):
            total += jnp.dot(part(ref, j), rights[j][...], preferred_element_type=F32)
        return total

    mid_ref[...] = chain(left_ref, g_refs).astype(BF16)
    product = chain(mid_ref, r_refs)
    out_ref[...] = product
    own = g_refs[0][...].astype(F32)
    rows = lax.broadcasted_iota(jnp.int32, sums_ref.shape, 0)
    sums_ref[...] = jnp.where(rows == 0, jnp.sum(product * product), jnp.sum(own * own))


def precondition(left, blocks, rights, *early):
    q, width = left.shape
    members = len(blocks)
    return pl.pallas_call(
        functools.partial(precond_kernel, members),
        out_shape=[
            jax.ShapeDtypeStruct((q, width), F32),
            jax.ShapeDtypeStruct((8, 128), F32),
        ],
        in_specs=[VMEM] * (1 + 2 * members) + [ANY] * len(early),
        out_specs=[VMEM, VMEM],
        scratch_shapes=[pltpu.VMEM((q, width), BF16)],
        compiler_params=params(16),
        cost_estimate=cost(4 * q * width * width, 4 * width * width + 4 * q * width),
        name="precondition",
    )(left, *blocks, *rights, *early)


def scale_kernel(entries, count, n, product_ref, *refs):
    sums_refs, outs = refs[:n], refs[-count:]
    me = lax.axis_index("fsdp")
    rows = outs[0].shape[0]
    total = sum(ref[...] for ref in sums_refs) / entries
    scale = jnp.sqrt(total[1:2, :1]) * lax.rsqrt(total[:1, :1] + 1e-06)
    for d, out_ref in enumerate(outs):
        part = product_ref[pl.ds(pl.multiple_of((me ^ d) * rows, rows), rows), :]
        out_ref[...] = (scale * part).astype(BF16)


def rescale(product, sums, entries, count, *early):
    rows, width = product.shape[0] // count, product.shape[1]
    return pl.pallas_call(
        functools.partial(scale_kernel, entries, count, len(sums)),
        out_shape=[jax.ShapeDtypeStruct((rows, width), BF16)] * count,
        in_specs=[VMEM] * (1 + len(sums)) + [HBM] * len(early),
        out_specs=[VMEM] * count,
        compiler_params=params(8),
        cost_estimate=cost(product.size, 6 * product.size),
        name="rescale",
    )(product, *sums, *map(in_hbm, early))


def start_statistic(rows_side, old_ref, g_refs, new_out, new_mem, sems):
    members = len(g_refs)
    member = lax.axis_index("rep")
    q, width = old_ref.shape
    step = 0.05 / width
    strip = pl.ds(pl.multiple_of(member * q, q), q)
    stores = []
    for j in range(members):
        if rows_side:
            cols = pl.ds(pl.multiple_of((member ^ j) * q, q), q)
            product = lax.dot_general(
                g_refs[0][...], g_refs[j][...], (((1,), (1,)), ((), ())), preferred_element_type=F32
            )
        else:
            cols = pl.ds(j * q, q)
            product = sum(
                lax.dot_general(
                    g[:, strip], g[:, cols], (((0,), (0,)), ((), ())), preferred_element_type=F32
                )
                for g in g_refs
            )
        new_mem[j] = 0.95 * old_ref[:, cols] + step * product
        stores.append(pltpu.make_async_copy(new_mem.at[j], new_out.at[:, cols], sems.at[j]))
        stores[-1].start()
    return stores


def stats_kernel(members, rows_side, old_ref, *refs):
    for store in start_statistic(rows_side, old_ref, refs[:members], *refs[members:]):
        store.wait()


def statistic(old, blocks, rows_side):
    q, width = old.shape
    members = len(blocks)
    return pl.pallas_call(
        functools.partial(stats_kernel, members, rows_side),
        out_shape=jax.ShapeDtypeStruct((q, width), F32),
        in_specs=[VMEM] * (1 + members),
        out_specs=HBM,
        scratch_shapes=[
            pltpu.VMEM((members, q, q), F32),
            pltpu.SemaphoreType.DMA((members,)),
        ],
        compiler_params=params(16),
        cost_estimate=cost(2 * q * width * width, 8 * q * width + 2 * width * width),
        name="left_statistic" if rows_side else "right_statistic",
    )(old, *blocks)


def stage_kernel(n, owner_ref, z_ref, x_ref, *refs):
    whole_refs, whole_outs = refs[:n], refs[-n - 6 : -6]
    z_out, x_out, block_out, owner_mem, block_mem, sems = refs[-6:]
    me = lax.axis_index("fsdp")
    count, _, width = z_out.shape
    index = pltpu.make_async_copy(owner_ref, owner_mem, sems.at[2, n])
    index.start()
    loads = [
        pltpu.make_async_copy(src, dst, sems.at[2, i])
        for i, (src, dst) in enumerate(zip(whole_refs, whole_outs))
    ]
    for load in loads:
        load.start()
    index.wait()
    invert(owner_mem, block_mem, count)
    for d in range(count):
        block = block_mem[me ^ d]
        block_out[pl.ds(d, 1), :] = jnp.full((1, block_out.shape[1]), block, jnp.int32)
        cols = pl.ds(pl.multiple_of(block * width, width), width)
        for i, (src, dst) in enumerate(((z_ref, z_out), (x_ref, x_out))):
            load = pltpu.make_async_copy(src.at[:, cols], dst.at[d], sems.at[i, d])
            load.start()
            loads.append(load)
    for load in loads:
        load.wait()


def stage(owner, z, x, wholes, count, *early):
    rows, width = z.shape[0], z.shape[1] // count
    n = len(wholes)
    moved = sum(2 * w.size * w.dtype.itemsize for w in wholes)
    return pl.pallas_call(
        functools.partial(stage_kernel, n),
        out_shape=[jax.ShapeDtypeStruct(w.shape, w.dtype) for w in wholes]
        + [
            jax.ShapeDtypeStruct((count, rows, width), F32),
            jax.ShapeDtypeStruct((count, rows, width), F32),
            jax.ShapeDtypeStruct((count, 128), jnp.int32),
        ],
        in_specs=[HBM] * (3 + n) + [ANY] * len(early),
        out_specs=[VMEM] * (n + 3),
        scratch_shapes=[
            pltpu.SMEM((count,), jnp.int32),
            pltpu.SMEM((count,), jnp.int32),
            pltpu.SemaphoreType.DMA((3, count)),
        ],
        compiler_params=params(8),
        cost_estimate=cost(0, 16 * z.size + moved),
        name="stage",
    )(*[in_hbm(a) for a in (owner, z, x, *wholes)], *early)


def update_kernel(distances, members, block_ref, z_ref, x_ref, *refs):
    n = len(distances)
    back, refs = refs[:n], refs[n:]
    stores = []
    if members:
        outs, (z_mem, x_mem, y_mem, sems) = refs[members + 1 : members + 4], refs[-6:-2]
        new_out = refs[members + 4]
        stores += start_statistic(False, refs[0], refs[1 : members + 1], new_out, *refs[-2:])
    else:
        outs, (z_mem, x_mem, y_mem, sems) = refs[3:6], refs[-4:]
    width = z_ref.shape[2]
    blocks = [block_ref[d, 0] for d in distances]
    for k, d in enumerate(distances):
        z_new = z_ref[d] - 0.2 * back[k][...].astype(F32)
        x_new = 0.75 * x_ref[d] + 0.25 * z_new
        z_mem[k] = z_new
        x_mem[k] = x_new
        y_mem[k] = (0.1 * z_new + 0.9 * x_new).astype(BF16)
        cols = pl.ds(pl.multiple_of(blocks[k] * width, width), width)
        for i, mem in enumerate((z_mem, x_mem, y_mem)):
            store = pltpu.make_async_copy(mem.at[k], outs[i].at[:, cols], sems.at[i, k])
            store.start()
            stores.append(store)
    for store in stores:
        store.wait()


def update(block, z, x, back, distances, held=None, stat=()):
    count, rows, width = z.shape
    flat = (rows, count * width)
    n = len(distances)
    fresh = held is None
    extra = []
    if stat:
        members, q = len(stat) - 1, stat[0].shape[0]
        extra = [pltpu.VMEM((members, q, q), F32), pltpu.SemaphoreType.DMA((members,))]
    return pl.pallas_call(
        functools.partial(update_kernel, distances, len(stat[1:])),
        out_shape=[
            jax.ShapeDtypeStruct(flat, F32),
            jax.ShapeDtypeStruct(flat, F32),
            jax.ShapeDtypeStruct(flat, BF16),
        ]
        + [jax.ShapeDtypeStruct(old.shape, F32) for old in stat[:1]],
        in_specs=[VMEM] * (3 + n) + [VMEM] * len(stat) + ([] if fresh else [HBM] * 3),
        out_specs=[HBM] * (4 if stat else 3),
        input_output_aliases={} if fresh else {3 + n + i: i for i in range(3)},
        scratch_shapes=[
            pltpu.VMEM((n, rows, width), F32),
            pltpu.VMEM((n, rows, width), F32),
            pltpu.VMEM((n, rows, width), BF16),
            pltpu.SemaphoreType.DMA((3, n)),
        ]
        + extra,
        compiler_params=params(16),
        cost_estimate=cost(8 * n * rows * width, 20 * n * rows * width),
        name="update",
    )(block, z, x, *[back[d] for d in distances], *stat, *([] if fresh else held))


def gather_members(own, members):
    bit = members // 2
    got = {0: own}
    while bit:
        for known in list(got):
            got[known ^ bit] = swap(got[known], "rep", members, bit)
        bit //= 2
    return [got[j] for j in range(members)]


def eight_by_four(flat, z, x, owner, stat_left, stat_right, root_left, root_right, count, members):
    def send(piece, d):
        return swap(piece, "fsdp", count, d)

    def far(piece):
        return swap(piece, "rep", members, 2)

    def sibling(piece):
        return swap(piece, "rep", members, 1)

    entries = float(stat_left.shape[1] ** 2)
    right_far = far(root_right)
    piece = route(flat, owner, count)
    got = {0: piece[0]}
    for d in (4, 5, 3, 1):
        got[d] = send(piece[d], d)
    got[2] = send(after(piece[2], got[3]), 2)
    got[7] = send(after(piece[7], got[1]), 7)
    got[6] = send(after(piece[6], got[4]), 6)
    first = half(got, FIRST, (4, 5, 1, 0))
    first_far = far(first)
    second = half(got, SECOND, (3, 2, 7, 6))
    second_far = far(second)
    wholes = (root_left, root_right, stat_left, stat_right)
    left, right, stat_left, stat_right, z, x, block = stage(owner, z, x, wholes, count, first, second)
    own = join(first, second, z)
    right_sibling = sibling(right)
    own_sibling = sibling(own)
    first_both, second_both = sibling(first_far), sibling(second_far)
    right_both = sibling(right_far)
    blocks = [own, own_sibling, join(first_far, second_far), join(first_both, second_both)]
    rights = [right, right_sibling, right_far, right_both]
    product, sums = precondition(left, blocks, rights)
    sums = [sums] + [swap(sums, "rep", members, j) for j in (1, 2, 3)]
    left_new = statistic(stat_left, blocks, True)
    piece = rescale(product, sums, entries, count, left_new)
    back = {0: piece[0]}
    for d in (4, 1, 5, 6, 7, 3, 2):
        back[d] = send(piece[d], d)
    *new, right_new = update(block, z, x, back, (4, 1, 5, 0), None, (stat_right, *blocks))
    for distances in ((6, 3), (7, 2)):
        new = update(block, z, x, back, distances, new)
    return (*new, left_new, right_new)


def any_shape(flat, z, x, owner, stat_left, stat_right, root_left, root_right, count, members):
    q, width = root_left.shape
    entries = float(width**2)
    rows = flat.shape[0]
    sent = jnp.take(flat.reshape(rows, count, width), jnp.argsort(owner), axis=1)
    sent = sent.transpose(1, 0, 2).astype(BF16)
    own = lax.all_to_all(sent, "fsdp", 0, 0, tiled=True).reshape(q, width)
    blocks = gather_members(own, members)
    rights = gather_members(root_right, members)
    product, sums = precondition(root_left, blocks, rights)
    total = sum([sums] + [swap(sums, "rep", members, j) for j in range(1, members)]) / entries
    scale = jnp.sqrt(total[1, 0]) * lax.rsqrt(total[0, 0] + 1e-06)
    back = (scale * product).astype(BF16).reshape(count, rows, width)
    back = lax.all_to_all(back, "fsdp", 0, 0, tiled=True)
    back = jnp.take(back, owner, axis=0).transpose(1, 0, 2).reshape(z.shape).astype(F32)
    z_new = z - 0.2 * back
    x_new = 0.75 * x + 0.25 * z_new
    y_new = (0.1 * z_new + 0.9 * x_new).astype(BF16)
    return (z_new, x_new, y_new, statistic(stat_left, blocks, True), statistic(stat_right, blocks, False))


def per_device(grad, z_params, x_params, owner, stat_left, stat_right, root_left, root_right):
    count = lax.axis_size("fsdp")
    members = lax.axis_size("rep")
    plan = eight_by_four if (count, members) == (8, 4) else any_shape
    held = (stat_left[0], stat_right[0], root_left[0], root_right[0])
    new = plan(grad[0], z_params[0], x_params[0], owner, *held, count, members)
    return tuple(part[None] for part in new)


def solution(mesh):
    flat = P("rep", "fsdp", None)
    held = P("fsdp", "rep", None)
    return jax.shard_map(
        per_device,
        mesh=mesh,
        in_specs=(flat, flat, flat, P(), held, held, held, held),
        out_specs=(flat, flat, flat, held, held),
        check_vma=False,
    )
```
